32 devices in a mesh: dp: 4 (over y, core), row: 2 (over x), col: 4 (over z).
Axes of the slice: x: 2, y: 2, z: 4, core: 2. Of those that a mesh axis runs over, the one named last changes fastest.
Arguments:
- gate_pre: bfloat16 [512, 14336], P('dp', 'row'), may hold values from -6 to 6
- up_pre: bfloat16 [512, 14336], P('dp', 'row'), may hold values from -6 to 6
- down_weight: bfloat16 [14336, 4096], P('row', 'col'), may hold values from -0.046875 to 0.046875
- cotangent: bfloat16 [512, 4096], P(('dp', 'row'), 'col'), may hold values from -6 to 6
Outputs:
- mixed: bfloat16 [512, 4096], P(('dp', 'row'), 'col')
- gate_grad: bfloat16 [512, 14336], P(('dp', 'col'), 'row')
- up_grad: bfloat16 [512, 14336], P(('dp', 'col'), 'row')
- weight_grad: float32 [14336, 4096], P(('row', 'dp'), 'col')
The draws below stay inside these ranges and needn't reach their ends.
All inputs are finite; a program needn't handle non-finite values.
Results may differ from the reference program's by a relative error of at most 0.017.
Values may be sent and summed in bfloat16 or wider, within the bound.
No kernel may reach another device: no remote copies, remote signals or barrier semaphores. Data moves between devices by JAX's collectives and lax.ppermute only.
A program may use at most 128 MiB of HBM per device.

```python
import jax
import jax.numpy as jnp
from jax import lax

D = 4096
FF = 14336
TOK = 128
TOKENS = 512
N_DP = 4
N_COL = 4


def level_of(stream_key, extent, pieces, smallest, top_value):
    loudness = 1.0
    for position, shards_of in pieces:
        heights = jax.random.uniform(jax.random.fold_in(jax.random.fold_in(stream_key, 6), position), (shards_of,), jnp.float32, smallest / len(pieces), top_value / len(pieces))
        loudness = loudness * jnp.repeat(jnp.exp(heights), extent[position] // shards_of).reshape((-1,) + (1,) * (len(extent) - 1 - position))
    return loudness


def gaussian(rng, shape, spread, bound, pieces=(), held_as=jnp.bfloat16):
    entries = jax.random.normal(rng, shape, jnp.float32) * spread
    if len(pieces) > 0:
        entries = level_of(rng, shape, pieces, -0.22, 0.18) * entries
    return jnp.clip(entries, min=-bound, max=bound).astype(held_as)


def setup_inputs(seed: int = 0) -> dict:
    splits = jax.random.split(jax.random.key(seed), 5)
    gate_pre = gaussian(splits[0], (TOKENS, FF), 1.0, 6.0, ((0, 4), (1, 2)))
    up_pre = gaussian(splits[1], (TOKENS, FF), 1.0, 6.0, ((0, 4), (1, 2)))
    down_weight = gaussian(splits[2], (FF, D), FF ** -0.5, 0.046875, ((0, 2), (1, 4)))
    cotangent = gaussian(splits[3], (TOKENS, D), 1.0, 6.0, ((0, 8), (1, 4)))
    return {"gate_pre": gate_pre, "up_pre": up_pre, "down_weight": down_weight, "cotangent": cotangent}


def reference(gate_pre, up_pre, down_weight, cotangent):
    gate_float = gate_pre.astype(jnp.float32)
    up_float = up_pre.astype(jnp.float32)
    sigmoid_gate = jax.nn.sigmoid(gate_float)
    activated = gate_float * sigmoid_gate
    hidden = (activated * up_float).astype(jnp.bfloat16)
    mixed = jnp.dot(hidden, down_weight, preferred_element_type=jnp.float32).astype(jnp.bfloat16)
    block_width = D // N_COL
    hidden_grad = jnp.zeros((gate_pre.shape[0], FF), jnp.float32)
    for block in range(N_COL):
        cot_block = cotangent[:, block * block_width:(block + 1) * block_width]
        weight_block = down_weight[:, block * block_width:(block + 1) * block_width]
        product = lax.dot_general(cot_block, weight_block, (((1,), (1,)), ((), ())), preferred_element_type=jnp.float32)
        rounded = lax.optimization_barrier(product.astype(jnp.bfloat16))
        hidden_grad = hidden_grad + rounded.astype(jnp.float32)
    gate_grad = (hidden_grad * up_float * sigmoid_gate * (1.0 + gate_float * (1.0 - sigmoid_gate))).astype(jnp.bfloat16)
    up_grad = (hidden_grad * activated).astype(jnp.bfloat16)

    def add_replica(replica, running):
        start = (replica * TOK).astype(jnp.int32)
        hidden_rows = lax.dynamic_slice_in_dim(hidden, start, TOK, 0)
        cot_rows = lax.dynamic_slice_in_dim(cotangent, start, TOK, 0)
        term = lax.dot_general(hidden_rows, cot_rows, (((0,), (0,)), ((), ())), preferred_element_type=jnp.float32)
        return running + term

    weight_sum = lax.fori_loop(jnp.int32(0), jnp.int32(N_DP), add_replica, jnp.zeros((FF, D), jnp.float32))
    weight_grad = weight_sum / jnp.float32(N_DP)
    return mixed, gate_grad, up_grad, weight_grad
```

```python
import jax
import jax.numpy as jnp
from jax import lax
from jax.sharding import PartitionSpec as P

SEND_ORDER = ((3, 2, 1, 0), (2, 0, 3, 1), (1, 3, 0, 2), (0, 1, 2, 3))
FAR_ENDS = ((0, 1), (3, 2))
MIDDLE = ((1, 2), (2, 1))
ROUND_TWO = ((0, 2), (2, 3), (3, 1), (1, 0))
ROUND_THREE = ((0, 1), (1, 3), (3, 2), (2, 0))


def gather_rows(cotangent):
    if lax.axis_size("row") != 2:
        return lax.all_gather(cotangent, "row", axis=0, tiled=True)
    other = lax.ppermute(cotangent, "row", [(0, 1), (1, 0)])
    first = lax.axis_index("row") == 0
    return jnp.concatenate(
        [jnp.where(first, cotangent, other), jnp.where(first, other, cotangent)], axis=0
    )


def scatter_rows(partial):
    if lax.axis_size("row") != 2:
        return lax.psum_scatter(partial, "row", scatter_dimension=0, tiled=True)
    half = partial.shape[0] // 2
    me = lax.axis_index("row")
    mine = lax.dynamic_slice_in_dim(partial, me * half, half, 0)
    theirs = lax.dynamic_slice_in_dim(partial, (1 - me) * half, half, 0)
    return mine + lax.ppermute(theirs, "row", [(0, 1), (1, 0)])


def hidden_gradient(cot_full, down_weight):
    def product(rows):
        return lax.dot_general(
            rows, down_weight, (((1,), (1,)), ((), ())), preferred_element_type=jnp.float32
        ).astype(jnp.bfloat16)

    if lax.axis_size("col") != 4:
        return lax.psum_scatter(
            product(cot_full), "col", scatter_dimension=0, tiled=True
        ).astype(jnp.float32)
    tokens = cot_full.shape[0] // 4
    order = jnp.asarray(SEND_ORDER, jnp.int32)[lax.axis_index("col")]
    blocks = [
        lax.dynamic_slice_in_dim(cot_full, order[i] * tokens, tokens, 0) for i in range(4)
    ]
    partial = product(jnp.concatenate(blocks, axis=0)).reshape(4, tokens, -1)
    transit = lax.ppermute(partial[0], "col", FAR_ENDS)
    middle = lax.ppermute(partial[0], "col", MIDDLE)
    second = lax.ppermute(partial[1], "col", ROUND_TWO)
    forward = (partial[2].astype(jnp.float32) + transit.astype(jnp.float32)).astype(jnp.bfloat16)
    third = lax.ppermute(forward, "col", ROUND_THREE)
    return (
        partial[3].astype(jnp.float32)
        + middle.astype(jnp.float32)
        + second.astype(jnp.float32)
        + third.astype(jnp.float32)
    )


def exchange_replicas(hidden, cot_full):
    if lax.axis_size("dp") != 4:
        return (
            lax.all_to_all(hidden, "dp", split_axis=1, concat_axis=0, tiled=True),
            lax.all_gather(cot_full, "dp", axis=0, tiled=True),
        )
    shard = hidden.shape[1] // 4
    me = lax.axis_index("dp")
    chip, core = me // 2, me % 2
    far = [(i, i ^ 2) for i in range(4)]
    near = [(i, i ^ 1) for i in range(4)]

    def part(index):
        return lax.dynamic_slice_in_dim(hidden, index * shard, shard, 1)

    from_far = lax.ppermute(
        lax.dynamic_slice_in_dim(hidden, (1 - chip) * 2 * shard, 2 * shard, 1), "dp", far
    )
    cot_far = lax.ppermute(cot_full, "dp", far)
    pair = jnp.concatenate([part(me), lax.dynamic_slice_in_dim(from_far, core * shard, shard, 1)], axis=0)
    to_near = jnp.concatenate(
        [part(me ^ 1), lax.dynamic_slice_in_dim(from_far, (1 - core) * shard, shard, 1)], axis=0
    )
    from_near = lax.ppermute(to_near, "dp", near)
    cot_pair = jnp.concatenate([cot_full, cot_far], axis=0)
    cot_near = lax.ppermute(cot_pair, "dp", near)
    return (
        jnp.concatenate([pair, from_near], axis=0),
        jnp.concatenate([cot_pair, cot_near], axis=0),
    )


def body(gate_pre, up_pre, down_weight, cotangent):
    gate_float = gate_pre.astype(jnp.float32)
    hidden = (gate_float * jax.nn.sigmoid(gate_float) * up_pre.astype(jnp.float32)).astype(
        jnp.bfloat16
    )
    cot_full = gather_rows(cotangent)
    hidden_share = hidden_gradient(cot_full, down_weight)
    mixed = scatter_rows(
        jnp.dot(hidden, down_weight, preferred_element_type=jnp.float32)
    ).astype(jnp.bfloat16)

    hidden_all, cot_all = exchange_replicas(hidden, cot_full)
    replicas = lax.axis_size("dp")
    weight_grad = lax.dot_general(
        hidden_all, cot_all, (((0,), (0,)), ((), ())), preferred_element_type=jnp.float32
    ) / jnp.float32(replicas)

    tok_rows = gate_pre.shape[0] // lax.axis_size("col")
    offset = lax.axis_index("col") * tok_rows
    gate_rows = lax.dynamic_slice_in_dim(gate_pre, offset, tok_rows, 0).astype(jnp.float32)
    up_rows = lax.dynamic_slice_in_dim(up_pre, offset, tok_rows, 0).astype(jnp.float32)
    sigmoid_rows = jax.nn.sigmoid(gate_rows)
    gate_grad = (
        hidden_share * up_rows * sigmoid_rows * (1.0 + gate_rows * (1.0 - sigmoid_rows))
    ).astype(jnp.bfloat16)
    up_grad = (hidden_share * gate_rows * sigmoid_rows).astype(jnp.bfloat16)
    return (mixed, gate_grad, up_grad, weight_grad)


def solution(mesh):
    placed = (P("dp", "row"), P("dp", "row"), P("row", "col"), P(("dp", "row"), "col"))
    return jax.shard_map(
        body,
        mesh=mesh,
        in_specs=placed,
        out_specs=(
            P(("dp", "row"), "col"),
            P(("dp", "col"), "row"),
            P(("dp", "col"), "row"),
            P(("row", "dp"), "col"),
        ),
        check_vma=False,
    )
```

```python
import functools

import jax
import jax.numpy as jnp
from jax import lax
from jax.experimental import pallas as pl
from jax.experimental.pallas import tpu as pltpu
from jax.sharding import PartitionSpec as P

SEND_ORDER = ((3, 2, 1, 0), (2, 0, 3, 1), (1, 3, 0, 2), (0, 1, 2, 3))
ENDS = ((0, 1), (1, 0), (2, 3), (3, 2))
MIDDLE = ((1, 2), (2, 1))
ROUND_TWO = ((0, 2), (2, 3), (3, 1), (1, 0))
ROUND_THREE = ((0, 1), (1, 3), (3, 2), (2, 0))
SWAP = ((0, 1), (1, 0))
FAR = ((0, 2), (1, 3), (2, 0), (3, 1))
NEAR = ((0, 1), (1, 0), (2, 3), (3, 2))

VMEM = pl.BlockSpec(memory_space=pltpu.VMEM)
HBM = pl.BlockSpec(memory_space=pltpu.HBM)
MIB = 2**20
CHUNK = 896
NO_COST = pl.CostEstimate(flops=0, bytes_accessed=0, transcendentals=0)


def after(value, *earlier):
    return lax.optimization_barrier((value,) + earlier)[0]


def in_hbm(array):
    return pltpu.with_memory_space_constraint(array, pltpu.HBM)


def in_vmem(array):
    return pltpu.with_memory_space_constraint(array, pltpu.VMEM)


def silu_product(gate, up):
    gate = gate.astype(jnp.float32)
    return (gate * jax.nn.sigmoid(gate) * up.astype(jnp.float32)).astype(jnp.bfloat16)


def shard_columns(ref, index, shard):
    return ref.at[:, pl.ds(pl.multiple_of(index * shard, shard), shard)]


def first_kernel(
    gate_hbm, up_hbm, weight_hbm, far_ref, weight_ref, gate_ref, up_ref, weight_sem, gate_sems, up_sems
):
    me = lax.axis_index("dp")
    tokens, shard = gate_ref.shape[1:]
    half = weight_ref.shape[0]

    def gate_copy(i):
        return pltpu.make_async_copy(
            shard_columns(gate_hbm, me ^ (3 - i), shard), gate_ref.at[i], gate_sems.at[i]
        )

    def up_copy(i):
        return pltpu.make_async_copy(
            shard_columns(up_hbm, me ^ (3 - i), shard), up_ref.at[i], up_sems.at[i]
        )

    load = pltpu.make_async_copy(weight_hbm.at[:half], weight_ref, weight_sem.at[0])
    for i in range(2):
        gate_copy(i).start()
        up_copy(i).start()
    load.start()
    for i in range(2):
        gate_copy(i).wait()
        up_copy(i).wait()
        far_ref[i * tokens : (i + 1) * tokens] = silu_product(gate_ref[i], up_ref[i])
    load.wait()


def hidden_far_and_weight(gate_pre, up_pre, down_weight):
    tokens, units = gate_pre.shape
    features = down_weight.shape[1]
    shard = units // 4
    return pl.pallas_call(
        first_kernel,
        in_specs=[HBM] * 3,
        out_specs=[VMEM] * 2,
        out_shape=[jax.ShapeDtypeStruct((2 * tokens, shard), jnp.bfloat16), pltpu.VMEM((units // 2, features), jnp.bfloat16)],
        scratch_shapes=[
            pltpu.VMEM((2, tokens, shard), jnp.bfloat16),
            pltpu.VMEM((2, tokens, shard), jnp.bfloat16),
            pltpu.SemaphoreType.DMA((1,)),
            pltpu.SemaphoreType.DMA((2,)),
            pltpu.SemaphoreType.DMA((2,)),
        ],
        compiler_params=pltpu.CompilerParams(vmem_limit_bytes=24 * MIB),
        cost_estimate=NO_COST,
        name="hidden_far",
    )(in_hbm(gate_pre), in_hbm(up_pre), in_hbm(down_weight))


def hidden_grad_kernel(
    own_ref, other_ref, low_ref, weight_hbm, full_ref, ends, middle, second, third, mine, ordered_ref, high_ref, sem
):
    units = low_ref.shape[0]
    load = pltpu.make_async_copy(weight_hbm.at[units:], high_ref, sem.at[0])
    load.start()
    half = own_ref.shape[0]
    tokens = half // 2
    top = lax.axis_index("row") == 0
    full_ref[:half] = jnp.where(top, own_ref[...], other_ref[...])
    full_ref[half:] = jnp.where(top, other_ref[...], own_ref[...])
    place = lax.axis_index("col")
    for i in range(4):
        block = jnp.int32(SEND_ORDER[0][i])
        for z in range(1, 4):
            block = jnp.where(place == z, jnp.int32(SEND_ORDER[z][i]), block)
        start = pl.multiple_of(block * tokens, tokens)
        ordered_ref[i * tokens : (i + 1) * tokens] = full_ref[pl.ds(start, tokens)]
    size = CHUNK if units % CHUNK == 0 else units
    for base, weight_ref in ((0, low_ref), (units, high_ref)):
        if base:
            load.wait()
        for start in range(0, units, size):
            product = lax.dot_general(
                weight_ref[start : start + size],
                ordered_ref[...],
                (((1,), (1,)), ((), ())),
                preferred_element_type=jnp.float32,
            )
            rounded = product.astype(jnp.bfloat16).T
            columns = slice(base + start, base + start + size)
            ends[:, columns] = rounded[:tokens]
            middle[:, columns] = rounded[:tokens]
            second[:, columns] = rounded[tokens : 2 * tokens]
            third[:, columns] = rounded[2 * tokens : 3 * tokens]
            mine[:, columns] = rounded[3 * tokens :]


def hidden_grad_parts(own, other, low, down_weight):
    half, depth = own.shape
    units = low.shape[0]
    part = jax.ShapeDtypeStruct((half // 2, 2 * units), jnp.bfloat16)
    return pl.pallas_call(
        hidden_grad_kernel,
        in_specs=[VMEM, VMEM, VMEM, HBM],
        out_specs=[VMEM] * 6,
        out_shape=[jax.ShapeDtypeStruct((2 * half, depth), jnp.bfloat16)] + [part] * 5,
        scratch_shapes=[
            pltpu.VMEM((2 * half, depth), jnp.bfloat16),
            pltpu.VMEM((units, depth), jnp.bfloat16),
            pltpu.SemaphoreType.DMA((1,)),
        ],
        compiler_params=pltpu.CompilerParams(vmem_limit_bytes=24 * MIB),
        cost_estimate=NO_COST,
        name="hidden_grad",
    )(own, other, in_vmem(low), in_hbm(down_weight))


def mixed_kernel(
    gate_hbm, up_hbm, weight_hbm, far_ref,
    near_ref, mine_ref, keep_ref, send_ref, gate_factor_ref, up_factor_ref,
    weight_ref, gate_ref, up_ref, gate_rows_ref, up_rows_ref, total_ref,
    weight_sems, gate_sems, up_sems, row_sems,
):
    me = lax.axis_index("dp")
    tokens, shard = mine_ref.shape
    tok_rows = gate_rows_ref.shape[0]
    places = (me ^ 3, me ^ 2, me ^ 1, me)
    refs = (far_ref.at[:tokens], far_ref.at[tokens:], near_ref, mine_ref)

    def gate_copy(i):
        return pltpu.make_async_copy(
            shard_columns(gate_hbm, places[2 + i], shard), gate_ref.at[i], gate_sems.at[i]
        )

    def up_copy(i):
        return pltpu.make_async_copy(
            shard_columns(up_hbm, places[2 + i], shard), up_ref.at[i], up_sems.at[i]
        )

    def weight_copy(i):
        start = pl.multiple_of(places[i] * shard, shard)
        return pltpu.make_async_copy(
            weight_hbm.at[pl.ds(start, shard)], weight_ref.at[i], weight_sems.at[i]
        )

    def row_copy(i):
        start = pl.multiple_of(lax.axis_index("col") * tok_rows, tok_rows)
        source, target = ((gate_hbm, gate_rows_ref), (up_hbm, up_rows_ref))[i]
        return pltpu.make_async_copy(source.at[pl.ds(start, tok_rows)], target, row_sems.at[i])

    for i in range(2):
        gate_copy(i).start()
        up_copy(i).start()
    for i in range(2):
        row_copy(i).start()
    for i in range(4):
        weight_copy(i).start()
    for i in range(2):
        gate_copy(i).wait()
        up_copy(i).wait()
        refs[2 + i][...] = silu_product(gate_ref[i], up_ref[i])
    row_copy(0).wait()
    row_copy(1).wait()
    units = gate_rows_ref.shape[1]
    for start in range(0, units, shard):
        columns = slice(start, start + shard)
        gate = gate_rows_ref[:, columns].astype(jnp.float32)
        sigmoid = jax.nn.sigmoid(gate)
        gate_factor_ref[:, columns] = (
            up_rows_ref[:, columns].astype(jnp.float32) * sigmoid * (1.0 + gate * (1.0 - sigmoid))
        )
        up_factor_ref[:, columns] = gate * sigmoid
    for i in range(4):
        weight_copy(i).wait()
        product = jnp.dot(refs[i][...], weight_ref[i], preferred_element_type=jnp.float32)
        if i == 0:
            total_ref[...] = product
        else:
            total_ref[...] += product
    half = tokens // 2
    row = lax.axis_index("row")
    keep_ref[...] = total_ref[pl.ds(pl.multiple_of(row * half, half), half)]
    send_ref[...] = total_ref[pl.ds(pl.multiple_of((1 - row) * half, half), half)]


def mixed_and_factors(gate_pre, up_pre, down_weight, far):
    tokens, units = gate_pre.shape
    shard = units // 4
    features = down_weight.shape[1]
    tok_rows = tokens // lax.axis_size("col")
    hidden = jax.ShapeDtypeStruct((tokens, shard), jnp.bfloat16)
    partial = jax.ShapeDtypeStruct((tokens // 2, features), jnp.float32)
    factor = jax.ShapeDtypeStruct((tok_rows, units), jnp.float32)
    return pl.pallas_call(
        mixed_kernel,
        in_specs=[HBM] * 3 + [VMEM],
        out_specs=[VMEM] * 6,
        out_shape=[hidden, hidden, partial, partial, factor, factor],
        scratch_shapes=[
            pltpu.VMEM((4, shard, features), jnp.bfloat16),
            pltpu.VMEM((2, tokens, shard), jnp.bfloat16),
            pltpu.VMEM((2, tokens, shard), jnp.bfloat16),
            pltpu.VMEM((tok_rows, units), jnp.bfloat16),
            pltpu.VMEM((tok_rows, units), jnp.bfloat16),
            pltpu.VMEM((tokens, features), jnp.float32),
            pltpu.SemaphoreType.DMA((4,)),
            pltpu.SemaphoreType.DMA((2,)),
            pltpu.SemaphoreType.DMA((2,)),
            pltpu.SemaphoreType.DMA((2,)),
        ],
        compiler_params=pltpu.CompilerParams(vmem_limit_bytes=32 * MIB),
        cost_estimate=NO_COST,
        name="mixed",
    )(in_hbm(gate_pre), in_hbm(up_pre), in_hbm(down_weight), far)


def weight_grad_kernel(scale, mine, far, near, both, cot_own, cot_far, cot_near, out):
    tokens = mine.shape[0]
    hidden = jnp.concatenate([mine[...], far[tokens:], near[...], both[...]], axis=0)
    cotangent = jnp.concatenate([cot_own[...], cot_far[...], cot_near[...]], axis=0)
    out[...] = lax.dot_general(
        hidden, cotangent, (((0,), (0,)), ((), ())), preferred_element_type=jnp.float32
    ) * jnp.float32(scale)


def weight_grad_shard(mine, far, near, both, cot_own, cot_far, cot_near):
    tokens, shard = mine.shape
    features = cot_own.shape[1]
    size = 896 if shard % 896 == 0 else shard

    def columns(array):
        return pl.BlockSpec((array.shape[0], size), lambda i: (0, i))

    def whole(array):
        return pl.BlockSpec(array.shape, lambda i: (0, 0))

    return pl.pallas_call(
        functools.partial(weight_grad_kernel, 0.25),
        grid=(shard // size,),
        in_specs=[columns(x) for x in (mine, far, near, both)]
        + [whole(x) for x in (cot_own, cot_far, cot_near)],
        out_specs=pl.BlockSpec((size, features), lambda i: (i, 0)),
        out_shape=jax.ShapeDtypeStruct((shard, features), jnp.float32),
        compiler_params=pltpu.CompilerParams(vmem_limit_bytes=24 * MIB),
        cost_estimate=NO_COST,
        name="weight_grad",
    )(mine, far, near, both, cot_own, cot_far, cot_near)


def gradient_factors(gate_pre, up_pre):
    tok_rows = gate_pre.shape[0] // lax.axis_size("col")
    offset = lax.axis_index("col") * tok_rows
    gate_rows = lax.dynamic_slice_in_dim(gate_pre, offset, tok_rows, 0).astype(jnp.float32)
    up_rows = lax.dynamic_slice_in_dim(up_pre, offset, tok_rows, 0).astype(jnp.float32)
    sigmoid_rows = jax.nn.sigmoid(gate_rows)
    return (
        up_rows * sigmoid_rows * (1.0 + gate_rows * (1.0 - sigmoid_rows)),
        gate_rows * sigmoid_rows,
    )


def body_line(gate_pre, up_pre, down_weight, cotangent):
    tokens = gate_pre.shape[0]
    cot_other = lax.ppermute(cotangent, "row", SWAP)
    cot_beside = lax.ppermute(cotangent, "dp", FAR)
    hidden_far, low = hidden_far_and_weight(gate_pre, up_pre, down_weight)

    cot_full, ends, middle, second, third, mine = hidden_grad_parts(
        after(cotangent, cot_beside), cot_other, low, down_weight
    )
    from_end = lax.ppermute(ends, "col", ENDS)
    from_middle = lax.ppermute(middle, "col", MIDDLE)
    from_second = lax.ppermute(second, "col", ROUND_TWO)
    far = lax.ppermute(after(hidden_far, mine), "dp", FAR)

    cot_across = lax.ppermute(after(cot_beside, mine), "row", SWAP)
    hidden_near, hidden_mine, keep, send, gate_factor, up_factor = mixed_and_factors(
        gate_pre, up_pre, down_weight, after(hidden_far, cot_across)
    )
    place = lax.axis_index("col")
    transit = jnp.where((place == 1) | (place == 2), from_end, jnp.zeros_like(from_end))
    forward = (
        after(third, from_middle, keep).astype(jnp.float32) + transit.astype(jnp.float32)
    ).astype(jnp.bfloat16)
    from_third = lax.ppermute(forward, "col", ROUND_THREE)

    top = lax.axis_index("row") == 0
    cot_far = jnp.concatenate(
        [jnp.where(top, cot_beside, cot_across), jnp.where(top, cot_across, cot_beside)], axis=0
    )
    cot_near = lax.ppermute(jnp.concatenate([cot_full, cot_far], axis=0), "dp", NEAR)
    near = lax.ppermute(after(hidden_near, forward), "dp", NEAR)
    mixed = (after(keep, forward) + lax.ppermute(after(send, forward), "row", SWAP)).astype(jnp.bfloat16)
    both = lax.ppermute(far[:tokens], "dp", NEAR)
    weight_grad = weight_grad_shard(hidden_mine, far, near, both, cot_full, cot_far, cot_near)

    so_far = (
        mine.astype(jnp.float32) + from_middle.astype(jnp.float32) + from_second.astype(jnp.float32)
    )
    so_far = lax.optimization_barrier((so_far, weight_grad))[0]
    hidden_share = so_far + after(from_third, weight_grad).astype(jnp.float32)
    gate_grad = (hidden_share * gate_factor).astype(jnp.bfloat16)
    up_grad = (hidden_share * up_factor).astype(jnp.bfloat16)
    return (mixed, gate_grad, up_grad, weight_grad)


def body_general(gate_pre, up_pre, down_weight, cotangent):
    hidden = silu_product(gate_pre, up_pre)
    cot_full = lax.all_gather(cotangent, "row", axis=0, tiled=True)
    hidden_share = lax.psum_scatter(
        lax.dot_general(
            cot_full, down_weight, (((1,), (1,)), ((), ())), preferred_element_type=jnp.float32
        ).astype(jnp.bfloat16),
        "col",
        scatter_dimension=0,
        tiled=True,
    ).astype(jnp.float32)
    mixed = lax.psum_scatter(
        jnp.dot(hidden, down_weight, preferred_element_type=jnp.float32),
        "row",
        scatter_dimension=0,
        tiled=True,
    ).astype(jnp.bfloat16)
    hidden_all = lax.all_to_all(hidden, "dp", split_axis=1, concat_axis=0, tiled=True)
    cot_all = lax.all_gather(cot_full, "dp", axis=0, tiled=True)
    weight_grad = lax.dot_general(
        hidden_all, cot_all, (((0,), (0,)), ((), ())), preferred_element_type=jnp.float32
    ) / jnp.float32(lax.axis_size("dp"))
    gate_factor, up_factor = gradient_factors(gate_pre, up_pre)
    gate_grad = (hidden_share * gate_factor).astype(jnp.bfloat16)
    up_grad = (hidden_share * up_factor).astype(jnp.bfloat16)
    return (mixed, gate_grad, up_grad, weight_grad)


def solution(mesh):
    sizes = (mesh.shape["dp"], mesh.shape["row"], mesh.shape["col"])
    placed = (P("dp", "row"), P("dp", "row"), P("row", "col"), P(("dp", "row"), "col"))
    return jax.shard_map(
        body_line if sizes == (4, 2, 4) else body_general,
        mesh=mesh,
        in_specs=placed,
        out_specs=(
            P(("dp", "row"), "col"),
            P(("dp", "col"), "row"),
            P(("dp", "col"), "row"),
            P(("row", "dp"), "col"),
        ),
        check_vma=False,
    )
```

```python
import functools

import jax
import jax.numpy as jnp
from jax import lax
from jax.experimental import pallas as pl
from jax.experimental.pallas import tpu as pltpu
from jax.sharding import PartitionSpec as P

SEND_ORDER = ((3, 2, 1, 0), (2, 0, 3, 1), (1, 3, 0, 2), (0, 1, 2, 3))
ENDS = ((0, 1), (1, 0), (2, 3), (3, 2))
MIDDLE = ((1, 2), (2, 1))
ROUND_TWO = ((0, 2), (2, 3), (3, 1), (1, 0))
ROUND_THREE = ((0, 1), (1, 3), (3, 2), (2, 0))
SWAP = ((0, 1), (1, 0))
FAR = ((0, 2), (1, 3), (2, 0), (3, 1))
NEAR = ((0, 1), (1, 0), (2, 3), (3, 2))

VMEM = pl.BlockSpec(memory_space=pltpu.VMEM)
HBM = pl.BlockSpec(memory_space=pltpu.HBM)
MIB = 2**20
CHUNK = 256
NO_COST = pl.CostEstimate(flops=0, bytes_accessed=0, transcendentals=0)


def after(value, *earlier):
    return lax.optimization_barrier((value,) + earlier)[0]


def in_hbm(array):
    return pltpu.with_memory_space_constraint(array, pltpu.HBM)


def in_vmem(array):
    return pltpu.with_memory_space_constraint(array, pltpu.VMEM)


def settled(array):
    top = lax.axis_index("row") == 0
    turned = lax.optimization_barrier(-array)
    turned = lax.optimization_barrier(jnp.where(top, -turned, turned))
    return lax.optimization_barrier(jnp.where(top, turned, -turned))


def silu_product(gate, up):
    gate = gate.astype(jnp.float32)
    return (gate * jax.nn.sigmoid(gate) * up.astype(jnp.float32)).astype(jnp.bfloat16)


def shard_columns(ref, index, shard):
    return ref.at[:, pl.ds(pl.multiple_of(index * shard, shard), shard)]


def first_kernel(
    gate_hbm, up_hbm, weight_hbm, far_ref, weight_ref, gate_ref, up_ref, weight_sem, gate_sems, up_sems
):
    me = lax.axis_index("dp")
    tokens, shard = gate_ref.shape[1:]
    half = weight_ref.shape[0]

    def gate_copy(i):
        return pltpu.make_async_copy(
            shard_columns(gate_hbm, me ^ (3 - i), shard), gate_ref.at[i], gate_sems.at[i]
        )

    def up_copy(i):
        return pltpu.make_async_copy(
            shard_columns(up_hbm, me ^ (3 - i), shard), up_ref.at[i], up_sems.at[i]
        )

    load = pltpu.make_async_copy(weight_hbm.at[:half], weight_ref, weight_sem.at[0])
    for i in range(2):
        gate_copy(i).start()
        up_copy(i).start()
    load.start()
    for i in range(2):
        gate_copy(i).wait()
        up_copy(i).wait()
        far_ref[i * tokens : (i + 1) * tokens] = silu_product(gate_ref[i], up_ref[i])
    load.wait()


def hidden_far_and_weight(gate_pre, up_pre, down_weight):
    tokens, units = gate_pre.shape
    features = down_weight.shape[1]
    shard = units // 4
    return pl.pallas_call(
        first_kernel,
        in_specs=[HBM] * 3,
        out_specs=[VMEM] * 2,
        out_shape=[jax.ShapeDtypeStruct((2 * tokens, shard), jnp.bfloat16), pltpu.VMEM((units // 2, features), jnp.bfloat16)],
        scratch_shapes=[
            pltpu.VMEM((2, tokens, shard), jnp.bfloat16),
            pltpu.VMEM((2, tokens, shard), jnp.bfloat16),
            pltpu.SemaphoreType.DMA((1,)),
            pltpu.SemaphoreType.DMA((2,)),
            pltpu.SemaphoreType.DMA((2,)),
        ],
        compiler_params=pltpu.CompilerParams(vmem_limit_bytes=24 * MIB),
        cost_estimate=NO_COST,
        name="hidden_far",
    )(in_hbm(gate_pre), in_hbm(up_pre), in_hbm(down_weight))


def hidden_grad_kernel(
    own_ref, other_ref, low_ref, weight_hbm, full_ref, ends, middle, second, third, mine, ordered_ref, high_ref, sem
):
    units = low_ref.shape[0]
    quarter = units // 2

    def load(i):
        rows = pl.ds(i * quarter, quarter)
        return pltpu.make_async_copy(
            weight_hbm.at[pl.ds(units + i * quarter, quarter)], high_ref.at[rows], sem.at[i]
        )

    load(0).start()
    load(1).start()
    half = own_ref.shape[0]
    tokens = half // 2
    top = lax.axis_index("row") == 0
    full_ref[:half] = jnp.where(top, own_ref[...], other_ref[...])
    full_ref[half:] = jnp.where(top, other_ref[...], own_ref[...])
    place = lax.axis_index("col")
    for i in range(4):
        block = jnp.int32(SEND_ORDER[0][i])
        for z in range(1, 4):
            block = jnp.where(place == z, jnp.int32(SEND_ORDER[z][i]), block)
        start = pl.multiple_of(block * tokens, tokens)
        ordered_ref[i * tokens : (i + 1) * tokens] = full_ref[pl.ds(start, tokens)]
    size = CHUNK if quarter % CHUNK == 0 else quarter
    for base, weight_ref in ((0, low_ref), (units, high_ref)):
        for start in range(0, units, size):
            if base and start % quarter == 0:
                load(start // quarter).wait()
            product = lax.dot_general(
                weight_ref[start : start + size],
                ordered_ref[...],
                (((1,), (1,)), ((), ())),
                preferred_element_type=jnp.float32,
            )
            rounded = product.astype(jnp.bfloat16).T
            columns = slice(base + start, base + start + size)
            ends[:, columns] = rounded[:tokens]
            middle[:, columns] = rounded[:tokens]
            second[:, columns] = rounded[tokens : 2 * tokens]
            third[:, columns] = rounded[2 * tokens : 3 * tokens]
            mine[:, columns] = rounded[3 * tokens :]


def hidden_grad_parts(own, other, low, down_weight):
    half, depth = own.shape
    units = low.shape[0]
    part = jax.ShapeDtypeStruct((half // 2, 2 * units), jnp.bfloat16)
    return pl.pallas_call(
        hidden_grad_kernel,
        in_specs=[VMEM, VMEM, VMEM, HBM],
        out_specs=[VMEM] * 6,
        out_shape=[jax.ShapeDtypeStruct((2 * half, depth), jnp.bfloat16)] + [part] * 5,
        scratch_shapes=[
            pltpu.VMEM((2 * half, depth), jnp.bfloat16),
            pltpu.VMEM((units, depth), jnp.bfloat16),
            pltpu.SemaphoreType.DMA((2,)),
        ],
        compiler_params=pltpu.CompilerParams(vmem_limit_bytes=24 * MIB),
        cost_estimate=NO_COST,
        name="hidden_grad",
    )(own, other, in_vmem(low), in_hbm(down_weight))


def mixed_kernel(
    gate_hbm, up_hbm, weight_hbm, far_ref,
    near_ref, mine_ref, keep_ref, send_ref, gate_factor_ref, up_factor_ref,
    weight_ref, gate_ref, up_ref, gate_rows_ref, up_rows_ref, total_ref,
    weight_sems, gate_sems, up_sems, row_sems,
):
    me = lax.axis_index("dp")
    tokens, shard = mine_ref.shape
    tok_rows = gate_rows_ref.shape[0]
    places = (me ^ 3, me ^ 2, me ^ 1, me)
    refs = (far_ref.at[:tokens], far_ref.at[tokens:], near_ref, mine_ref)

    def gate_copy(i):
        return pltpu.make_async_copy(
            shard_columns(gate_hbm, places[2 + i], shard), gate_ref.at[i], gate_sems.at[i]
        )

    def up_copy(i):
        return pltpu.make_async_copy(
            shard_columns(up_hbm, places[2 + i], shard), up_ref.at[i], up_sems.at[i]
        )

    def weight_copy(i):
        start = pl.multiple_of(places[i] * shard, shard)
        return pltpu.make_async_copy(
            weight_hbm.at[pl.ds(start, shard)], weight_ref.at[i], weight_sems.at[i]
        )

    def row_copy(i):
        start = pl.multiple_of(lax.axis_index("col") * tok_rows, tok_rows)
        source, target = ((gate_hbm, gate_rows_ref), (up_hbm, up_rows_ref))[i]
        return pltpu.make_async_copy(source.at[pl.ds(start, tok_rows)], target, row_sems.at[i])

    for i in range(2):
        gate_copy(i).start()
        up_copy(i).start()
    for i in range(2):
        row_copy(i).start()
    for i in range(4):
        weight_copy(i).start()
    for i in range(2):
        gate_copy(i).wait()
        up_copy(i).wait()
        refs[2 + i][...] = silu_product(gate_ref[i], up_ref[i])
    row_copy(0).wait()
    row_copy(1).wait()
    units = gate_rows_ref.shape[1]
    for start in range(0, units, shard):
        columns = slice(start, start + shard)
        gate = gate_rows_ref[:, columns].astype(jnp.float32)
        sigmoid = jax.nn.sigmoid(gate)
        gate_factor_ref[:, columns] = (
            up_rows_ref[:, columns].astype(jnp.float32) * sigmoid * (1.0 + gate * (1.0 - sigmoid))
        )
        up_factor_ref[:, columns] = gate * sigmoid
    for i in range(4):
        weight_copy(i).wait()
        product = jnp.dot(refs[i][...], weight_ref[i], preferred_element_type=jnp.float32)
        if i == 0:
            total_ref[...] = product
        else:
            total_ref[...] += product
    half = tokens // 2
    row = lax.axis_index("row")
    keep_ref[...] = total_ref[pl.ds(pl.multiple_of(row * half, half), half)]
    send_ref[...] = total_ref[pl.ds(pl.multiple_of((1 - row) * half, half), half)]


def mixed_and_factors(gate_pre, up_pre, down_weight, far):
    tokens, units = gate_pre.shape
    shard = units // 4
    features = down_weight.shape[1]
    tok_rows = tokens // lax.axis_size("col")
    hidden = jax.ShapeDtypeStruct((tokens, shard), jnp.bfloat16)
    partial = jax.ShapeDtypeStruct((tokens // 2, features), jnp.float32)
    factor = jax.ShapeDtypeStruct((tok_rows, units), jnp.float32)
    return pl.pallas_call(
        mixed_kernel,
        in_specs=[HBM] * 3 + [VMEM],
        out_specs=[VMEM] * 6,
        out_shape=[hidden, hidden, partial, partial, factor, factor],
        scratch_shapes=[
            pltpu.VMEM((4, shard, features), jnp.bfloat16),
            pltpu.VMEM((2, tokens, shard), jnp.bfloat16),
            pltpu.VMEM((2, tokens, shard), jnp.bfloat16),
            pltpu.VMEM((tok_rows, units), jnp.bfloat16),
            pltpu.VMEM((tok_rows, units), jnp.bfloat16),
            pltpu.VMEM((tokens, features), jnp.float32),
            pltpu.SemaphoreType.DMA((4,)),
            pltpu.SemaphoreType.DMA((2,)),
            pltpu.SemaphoreType.DMA((2,)),
            pltpu.SemaphoreType.DMA((2,)),
        ],
        compiler_params=pltpu.CompilerParams(vmem_limit_bytes=32 * MIB),
        cost_estimate=NO_COST,
        name="mixed",
    )(in_hbm(gate_pre), in_hbm(up_pre), in_hbm(down_weight), far)


def weight_grad_kernel(scale, mine, far, near, both, cot_own, cot_far, cot_near, out):
    tokens = mine.shape[0]
    hidden = jnp.concatenate([mine[...], far[tokens:], near[...], both[...]], axis=0)
    cotangent = jnp.concatenate([cot_own[...], cot_far[...], cot_near[...]], axis=0)
    out[...] = lax.dot_general(
        hidden, cotangent, (((0,), (0,)), ((), ())), preferred_element_type=jnp.float32
    ) * jnp.float32(scale)


def weight_grad_shard(mine, far, near, both, cot_own, cot_far, cot_near):
    tokens, shard = mine.shape
    features = cot_own.shape[1]
    size = 896 if shard % 896 == 0 else shard

    def columns(array):
        return pl.BlockSpec((array.shape[0], size), lambda i: (0, i))

    def whole(array):
        return pl.BlockSpec(array.shape, lambda i: (0, 0))

    return pl.pallas_call(
        functools.partial(weight_grad_kernel, 0.25),
        grid=(shard // size,),
        in_specs=[columns(x) for x in (mine, far, near, both)]
        + [whole(x) for x in (cot_own, cot_far, cot_near)],
        out_specs=pl.BlockSpec((size, features), lambda i: (i, 0)),
        out_shape=jax.ShapeDtypeStruct((shard, features), jnp.float32),
        compiler_params=pltpu.CompilerParams(vmem_limit_bytes=24 * MIB),
        cost_estimate=NO_COST,
        name="weight_grad",
    )(mine, far, near, both, cot_own, cot_far, cot_near)


def gradient_factors(gate_pre, up_pre):
    tok_rows = gate_pre.shape[0] // lax.axis_size("col")
    offset = lax.axis_index("col") * tok_rows
    gate_rows = lax.dynamic_slice_in_dim(gate_pre, offset, tok_rows, 0).astype(jnp.float32)
    up_rows = lax.dynamic_slice_in_dim(up_pre, offset, tok_rows, 0).astype(jnp.float32)
    sigmoid_rows = jax.nn.sigmoid(gate_rows)
    return (
        up_rows * sigmoid_rows * (1.0 + gate_rows * (1.0 - sigmoid_rows)),
        gate_rows * sigmoid_rows,
    )


def body_line(gate_pre, up_pre, down_weight, cotangent):
    tokens = gate_pre.shape[0]
    cot_other = lax.ppermute(cotangent, "row", SWAP)
    hidden_far, low = hidden_far_and_weight(gate_pre, up_pre, down_weight)

    cot_full, ends, middle, second, third, mine = hidden_grad_parts(
        cotangent, cot_other, low, down_weight
    )
    from_end = lax.ppermute(ends, "col", ENDS)
    from_middle = lax.ppermute(middle, "col", MIDDLE)
    from_second = lax.ppermute(second, "col", ROUND_TWO)
    far = lax.ppermute(after(hidden_far, mine), "dp", FAR)

    cot_far = lax.ppermute(after(cot_full, mine), "dp", FAR)
    hidden_near, hidden_mine, keep, send, gate_factor, up_factor = mixed_and_factors(
        gate_pre, up_pre, down_weight, after(hidden_far, cot_far)
    )
    place = lax.axis_index("col")
    transit = jnp.where((place == 1) | (place == 2), from_end, jnp.zeros_like(from_end))
    forward = (
        after(third, from_middle, keep).astype(jnp.float32) + transit.astype(jnp.float32)
    ).astype(jnp.bfloat16)
    from_third = lax.ppermute(forward, "col", ROUND_THREE)

    cot_far = settled(cot_far)
    cot_near = lax.ppermute(jnp.concatenate([cot_full, cot_far], axis=0), "dp", NEAR)
    near = lax.ppermute(after(hidden_near, forward), "dp", NEAR)
    mixed = (after(keep, forward) + lax.ppermute(after(send, forward), "row", SWAP)).astype(jnp.bfloat16)
    both = lax.ppermute(far[:tokens], "dp", NEAR)
    weight_grad = weight_grad_shard(hidden_mine, far, near, both, cot_full, cot_far, cot_near)

    so_far = (
        mine.astype(jnp.float32) + from_middle.astype(jnp.float32) + from_second.astype(jnp.float32)
    )
    so_far = lax.optimization_barrier((so_far, weight_grad))[0]
    hidden_share = so_far + after(from_third, weight_grad).astype(jnp.float32)
    gate_grad = (hidden_share * gate_factor).astype(jnp.bfloat16)
    up_grad = (hidden_share * up_factor).astype(jnp.bfloat16)
    return (mixed, gate_grad, up_grad, weight_grad)


def body_general(gate_pre, up_pre, down_weight, cotangent):
    hidden = silu_product(gate_pre, up_pre)
    cot_full = lax.all_gather(cotangent, "row", axis=0, tiled=True)
    hidden_share = lax.psum_scatter(
        lax.dot_general(
            cot_full, down_weight, (((1,), (1,)), ((), ())), preferred_element_type=jnp.float32
        ).astype(jnp.bfloat16),
        "col",
        scatter_dimension=0,
        tiled=True,
    ).astype(jnp.float32)
    mixed = lax.psum_scatter(
        jnp.dot(hidden, down_weight, preferred_element_type=jnp.float32),
        "row",
        scatter_dimension=0,
        tiled=True,
    ).astype(jnp.bfloat16)
    hidden_all = lax.all_to_all(hidden, "dp", split_axis=1, concat_axis=0, tiled=True)
    cot_all = lax.all_gather(cot_full, "dp", axis=0, tiled=True)
    weight_grad = lax.dot_general(
        hidden_all, cot_all, (((0,), (0,)), ((), ())), preferred_element_type=jnp.float32
    ) / jnp.float32(lax.axis_size("dp"))
    gate_factor, up_factor = gradient_factors(gate_pre, up_pre)
    gate_grad = (hidden_share * gate_factor).astype(jnp.bfloat16)
    up_grad = (hidden_share * up_factor).astype(jnp.bfloat16)
    return (mixed, gate_grad, up_grad, weight_grad)


def solution(mesh):
    sizes = (mesh.shape["dp"], mesh.shape["row"], mesh.shape["col"])
    placed = (P("dp", "row"), P("dp", "row"), P("row", "col"), P(("dp", "row"), "col"))
    return jax.shard_map(
        body_line if sizes == (4, 2, 4) else body_general,
        mesh=mesh,
        in_specs=placed,
        out_specs=(
            P(("dp", "row"), "col"),
            P(("dp", "col"), "row"),
            P(("dp", "col"), "row"),
            P(("row", "dp"), "col"),
        ),
        check_vma=False,
    )
```

```python
import functools

import jax
import jax.numpy as jnp
from jax import lax
from jax.experimental import pallas as pl
from jax.experimental.pallas import tpu as pltpu
from jax.sharding import PartitionSpec as P

SEND_ORDER = ((3, 2, 1, 0), (2, 0, 3, 1), (1, 3, 0, 2), (0, 1, 2, 3))
ENDS = ((0, 1), (1, 0), (2, 3), (3, 2))
MIDDLE = ((1, 2), (2, 1))
ROUND_TWO = ((0, 2), (2, 3), (3, 1), (1, 0))
ROUND_THREE = ((0, 1), (1, 3), (3, 2), (2, 0))
SWAP = ((0, 1), (1, 0))
FAR = ((0, 2), (1, 3), (2, 0), (3, 1))
ACROSS = ((0, 3), (1, 2), (2, 1), (3, 0))
NEAR = ((0, 1), (1, 0), (2, 3), (3, 2))

VMEM = pl.BlockSpec(memory_space=pltpu.VMEM)
HBM = pl.BlockSpec(memory_space=pltpu.HBM)
MIB = 2**20
CHUNK = 256
WEIGHT_GRAD_PIECES = 7
NO_COST = pl.CostEstimate(flops=0, bytes_accessed=0, transcendentals=0)


def after(value, *earlier):
    return lax.optimization_barrier((value,) + earlier)[0]


def in_hbm(array):
    return pltpu.with_memory_space_constraint(array, pltpu.HBM)


def in_vmem(array):
    return pltpu.with_memory_space_constraint(array, pltpu.VMEM)


def silu_product(gate, up):
    gate = gate.astype(jnp.float32)
    return (gate * jax.nn.sigmoid(gate) * up.astype(jnp.float32)).astype(jnp.bfloat16)


def shard_columns(ref, index, shard):
    return ref.at[:, pl.ds(pl.multiple_of(index * shard, shard), shard)]


def first_kernel(
    gate_hbm, up_hbm, weight_hbm, across_ref, beside_ref, weight_ref, gate_ref, up_ref, weight_sem, gate_sems, up_sems
):
    me = lax.axis_index("dp")
    shard = gate_ref.shape[2]
    half = weight_ref.shape[0]

    def gate_copy(i):
        return pltpu.make_async_copy(
            shard_columns(gate_hbm, me ^ (3 - i), shard), gate_ref.at[i], gate_sems.at[i]
        )

    def up_copy(i):
        return pltpu.make_async_copy(
            shard_columns(up_hbm, me ^ (3 - i), shard), up_ref.at[i], up_sems.at[i]
        )

    load = pltpu.make_async_copy(weight_hbm.at[:half], weight_ref, weight_sem.at[0])
    for i in range(2):
        gate_copy(i).start()
        up_copy(i).start()
    load.start()
    for i, hidden_ref in enumerate((across_ref, beside_ref)):
        gate_copy(i).wait()
        up_copy(i).wait()
        hidden_ref[...] = silu_product(gate_ref[i], up_ref[i])
    load.wait()


def hidden_far_and_weight(gate_pre, up_pre, down_weight):
    tokens, units = gate_pre.shape
    features = down_weight.shape[1]
    shard = units // 4
    hidden = jax.ShapeDtypeStruct((tokens, shard), jnp.bfloat16)
    return pl.pallas_call(
        first_kernel,
        in_specs=[HBM] * 3,
        out_specs=[VMEM] * 3,
        out_shape=[hidden, hidden, pltpu.VMEM((units // 2, features), jnp.bfloat16)],
        scratch_shapes=[
            pltpu.VMEM((2, tokens, shard), jnp.bfloat16),
            pltpu.VMEM((2, tokens, shard), jnp.bfloat16),
            pltpu.SemaphoreType.DMA((1,)),
            pltpu.SemaphoreType.DMA((2,)),
            pltpu.SemaphoreType.DMA((2,)),
        ],
        compiler_params=pltpu.CompilerParams(vmem_limit_bytes=24 * MIB),
        cost_estimate=NO_COST,
        name="hidden_far",
    )(in_hbm(gate_pre), in_hbm(up_pre), in_hbm(down_weight))


def hidden_grad_kernel(
    own_ref, other_ref, low_ref, weight_hbm, full_ref, ends, middle, second, third, mine, ordered_ref, high_ref, sem
):
    units = low_ref.shape[0]
    quarter = units // 2

    def load(i):
        rows = pl.ds(i * quarter, quarter)
        return pltpu.make_async_copy(
            weight_hbm.at[pl.ds(units + i * quarter, quarter)], high_ref.at[rows], sem.at[i]
        )

    load(0).start()
    load(1).start()
    half = own_ref.shape[0]
    tokens = half // 2
    top = lax.axis_index("row") == 0
    full_ref[:half] = jnp.where(top, own_ref[...], other_ref[...])
    full_ref[half:] = jnp.where(top, other_ref[...], own_ref[...])
    place = lax.axis_index("col")
    for i in range(4):
        block = jnp.int32(SEND_ORDER[0][i])
        for z in range(1, 4):
            block = jnp.where(place == z, jnp.int32(SEND_ORDER[z][i]), block)
        start = pl.multiple_of(block * tokens, tokens)
        ordered_ref[i * tokens : (i + 1) * tokens] = full_ref[pl.ds(start, tokens)]
    size = CHUNK if quarter % CHUNK == 0 else quarter
    for base, weight_ref in ((0, low_ref), (units, high_ref)):
        for start in range(0, units, size):
            if base and start % quarter == 0:
                load(start // quarter).wait()
            product = lax.dot_general(
                weight_ref[start : start + size],
                ordered_ref[...],
                (((1,), (1,)), ((), ())),
                preferred_element_type=jnp.float32,
            )
            rounded = product.astype(jnp.bfloat16).T
            columns = slice(base + start, base + start + size)
            ends[:, columns] = rounded[:tokens]
            middle[:, columns] = rounded[:tokens]
            second[:, columns] = rounded[tokens : 2 * tokens]
            third[:, columns] = rounded[2 * tokens : 3 * tokens]
            mine[:, columns] = rounded[3 * tokens :]


def hidden_grad_parts(own, other, low, down_weight):
    half, depth = own.shape
    units = low.shape[0]
    part = jax.ShapeDtypeStruct((half // 2, 2 * units), jnp.bfloat16)
    return pl.pallas_call(
        hidden_grad_kernel,
        in_specs=[VMEM, VMEM, VMEM, HBM],
        out_specs=[VMEM] * 6,
        out_shape=[jax.ShapeDtypeStruct((2 * half, depth), jnp.bfloat16)] + [part] * 5,
        scratch_shapes=[
            pltpu.VMEM((2 * half, depth), jnp.bfloat16),
            pltpu.VMEM((units, depth), jnp.bfloat16),
            pltpu.SemaphoreType.DMA((2,)),
        ],
        compiler_params=pltpu.CompilerParams(vmem_limit_bytes=24 * MIB),
        cost_estimate=NO_COST,
        name="hidden_grad",
    )(own, other, in_vmem(low), in_hbm(down_weight))


def mixed_kernel(
    gate_hbm, up_hbm, weight_hbm, across_ref, beside_ref,
    near_ref, mine_ref, keep_ref, send_ref, gate_factor_ref, up_factor_ref,
    weight_ref, gate_ref, up_ref, gate_rows_ref, up_rows_ref, total_ref,
    weight_sems, gate_sems, up_sems, row_sems,
):
    me = lax.axis_index("dp")
    tokens, shard = mine_ref.shape
    tok_rows = gate_rows_ref.shape[0]
    places = (me ^ 3, me ^ 2, me ^ 1, me)
    refs = (across_ref, beside_ref, near_ref, mine_ref)

    def gate_copy(i):
        return pltpu.make_async_copy(
            shard_columns(gate_hbm, places[2 + i], shard), gate_ref.at[i], gate_sems.at[i]
        )

    def up_copy(i):
        return pltpu.make_async_copy(
            shard_columns(up_hbm, places[2 + i], shard), up_ref.at[i], up_sems.at[i]
        )

    def weight_copy(i):
        start = pl.multiple_of(places[i] * shard, shard)
        return pltpu.make_async_copy(
            weight_hbm.at[pl.ds(start, shard)], weight_ref.at[i], weight_sems.at[i]
        )

    def row_copy(i):
        start = pl.multiple_of(lax.axis_index("col") * tok_rows, tok_rows)
        source, target = ((gate_hbm, gate_rows_ref), (up_hbm, up_rows_ref))[i]
        return pltpu.make_async_copy(source.at[pl.ds(start, tok_rows)], target, row_sems.at[i])

    for i in range(2):
        gate_copy(i).start()
        up_copy(i).start()
    for i in range(2):
        row_copy(i).start()
    for i in range(4):
        weight_copy(i).start()
    for i in range(2):
        gate_copy(i).wait()
        up_copy(i).wait()
        refs[2 + i][...] = silu_product(gate_ref[i], up_ref[i])
    row_copy(0).wait()
    row_copy(1).wait()
    units = gate_rows_ref.shape[1]
    for start in range(0, units, shard):
        columns = slice(start, start + shard)
        gate = gate_rows_ref[:, columns].astype(jnp.float32)
        sigmoid = jax.nn.sigmoid(gate)
        gate_factor_ref[:, columns] = (
            up_rows_ref[:, columns].astype(jnp.float32) * sigmoid * (1.0 + gate * (1.0 - sigmoid))
        )
        up_factor_ref[:, columns] = gate * sigmoid
    for i in range(4):
        weight_copy(i).wait()
        product = jnp.dot(refs[i][...], weight_ref[i], preferred_element_type=jnp.float32)
        if i == 0:
            total_ref[...] = product
        else:
            total_ref[...] += product
    half = tokens // 2
    row = lax.axis_index("row")
    keep_ref[...] = total_ref[pl.ds(pl.multiple_of(row * half, half), half)]
    send_ref[...] = total_ref[pl.ds(pl.multiple_of((1 - row) * half, half), half)]


def mixed_and_factors(gate_pre, up_pre, down_weight, across, beside):
    tokens, units = gate_pre.shape
    shard = units // 4
    features = down_weight.shape[1]
    tok_rows = tokens // lax.axis_size("col")
    hidden = jax.ShapeDtypeStruct((tokens, shard), jnp.bfloat16)
    partial = jax.ShapeDtypeStruct((tokens // 2, features), jnp.float32)
    factor = jax.ShapeDtypeStruct((tok_rows, units), jnp.float32)
    return pl.pallas_call(
        mixed_kernel,
        in_specs=[HBM] * 3 + [VMEM] * 2,
        out_specs=[VMEM] * 6,
        out_shape=[hidden, hidden, partial, partial, factor, factor],
        scratch_shapes=[
            pltpu.VMEM((4, shard, features), jnp.bfloat16),
            pltpu.VMEM((2, tokens, shard), jnp.bfloat16),
            pltpu.VMEM((2, tokens, shard), jnp.bfloat16),
            pltpu.VMEM((tok_rows, units), jnp.bfloat16),
            pltpu.VMEM((tok_rows, units), jnp.bfloat16),
            pltpu.VMEM((tokens, features), jnp.float32),
            pltpu.SemaphoreType.DMA((4,)),
            pltpu.SemaphoreType.DMA((2,)),
            pltpu.SemaphoreType.DMA((2,)),
            pltpu.SemaphoreType.DMA((2,)),
        ],
        compiler_params=pltpu.CompilerParams(vmem_limit_bytes=32 * MIB),
        cost_estimate=NO_COST,
        name="mixed",
    )(in_hbm(gate_pre), in_hbm(up_pre), in_hbm(down_weight), across, beside)


def weight_grad_kernel(scale, hidden_ref, cot_own, cot_far, cot_near, out_hbm, buffer, sems):
    cotangent = jnp.concatenate([cot_own[...], cot_far[...], cot_near[...]], axis=0)
    shard = hidden_ref.shape[1]
    size = shard // sems.shape[0]

    def copy_out(i):
        rows = pl.ds(i * size, size)
        return pltpu.make_async_copy(buffer.at[rows], out_hbm.at[rows], sems.at[i])

    for i in range(sems.shape[0]):
        buffer[i * size : (i + 1) * size] = lax.dot_general(
            hidden_ref[:, i * size : (i + 1) * size],
            cotangent,
            (((0,), (0,)), ((), ())),
            preferred_element_type=jnp.float32,
        ) * jnp.float32(scale)
        copy_out(i).start()
    for i in range(sems.shape[0]):
        copy_out(i).wait()


def weight_grad_shard(hidden, cot_own, cot_far, cot_near):
    shard = hidden.shape[1]
    features = cot_own.shape[1]
    pieces = WEIGHT_GRAD_PIECES if shard % (128 * WEIGHT_GRAD_PIECES) == 0 else 1
    return pl.pallas_call(
        functools.partial(weight_grad_kernel, 0.25),
        in_specs=[VMEM] * 4,
        out_specs=HBM,
        out_shape=jax.ShapeDtypeStruct((shard, features), jnp.float32),
        scratch_shapes=[
            pltpu.VMEM((shard, features), jnp.float32),
            pltpu.SemaphoreType.DMA((pieces,)),
        ],
        compiler_params=pltpu.CompilerParams(vmem_limit_bytes=24 * MIB),
        cost_estimate=NO_COST,
        name="weight_grad",
    )(hidden, cot_own, cot_far, cot_near)


def gradient_factors(gate_pre, up_pre):
    tok_rows = gate_pre.shape[0] // lax.axis_size("col")
    offset = lax.axis_index("col") * tok_rows
    gate_rows = lax.dynamic_slice_in_dim(gate_pre, offset, tok_rows, 0).astype(jnp.float32)
    up_rows = lax.dynamic_slice_in_dim(up_pre, offset, tok_rows, 0).astype(jnp.float32)
    sigmoid_rows = jax.nn.sigmoid(gate_rows)
    return (
        up_rows * sigmoid_rows * (1.0 + gate_rows * (1.0 - sigmoid_rows)),
        gate_rows * sigmoid_rows,
    )


def body_line(gate_pre, up_pre, down_weight, cotangent):
    cot_other = lax.ppermute(cotangent, "row", SWAP)
    hidden_across, hidden_beside, low = hidden_far_and_weight(gate_pre, up_pre, down_weight)

    cot_full, ends, middle, second, third, mine = hidden_grad_parts(
        cotangent, cot_other, low, down_weight
    )
    from_end = lax.ppermute(ends, "col", ENDS)
    from_middle = lax.ppermute(middle, "col", MIDDLE)
    from_second = lax.ppermute(second, "col", ROUND_TWO)
    across = lax.ppermute(after(hidden_across, mine), "dp", ACROSS)
    beside = lax.ppermute(after(hidden_beside, mine), "dp", FAR)

    cot_far = lax.ppermute(after(cot_full, mine), "dp", FAR)
    place = lax.axis_index("col")
    transit = jnp.where((place == 1) | (place == 2), from_end, jnp.zeros_like(from_end))
    forward = (
        after(third, from_middle).astype(jnp.float32) + transit.astype(jnp.float32)
    ).astype(jnp.bfloat16)
    from_third = lax.ppermute(forward, "col", ROUND_THREE)
    hidden_near, hidden_mine, keep, send, gate_factor, up_factor = mixed_and_factors(
        gate_pre, up_pre, down_weight, after(hidden_across, cot_far, forward), hidden_beside
    )

    cot_near = lax.ppermute(jnp.concatenate([cot_full, cot_far], axis=0), "dp", NEAR)
    near = lax.ppermute(after(hidden_near, forward, beside), "dp", NEAR)
    other_half = lax.ppermute(after(send, forward), "row", SWAP)
    hidden_all = lax.optimization_barrier(
        jnp.concatenate([hidden_mine, beside, near, across], axis=0)
    )
    weight_grad = weight_grad_shard(hidden_all, cot_full, cot_far, cot_near)

    mixed = (after(keep, weight_grad) + other_half).astype(jnp.bfloat16)
    so_far = (
        mine.astype(jnp.float32) + from_middle.astype(jnp.float32) + from_second.astype(jnp.float32)
    )
    so_far = lax.optimization_barrier((so_far, weight_grad))[0]
    hidden_share = so_far + after(from_third, weight_grad, mixed).astype(jnp.float32)
    gate_grad = (hidden_share * gate_factor).astype(jnp.bfloat16)
    up_grad = (hidden_share * up_factor).astype(jnp.bfloat16)
    return (mixed, gate_grad, up_grad, weight_grad)


def body_general(gate_pre, up_pre, down_weight, cotangent):
    hidden = silu_product(gate_pre, up_pre)
    cot_full = lax.all_gather(cotangent, "row", axis=0, tiled=True)
    hidden_share = lax.psum_scatter(
        lax.dot_general(
            cot_full, down_weight, (((1,), (1,)), ((), ())), preferred_element_type=jnp.float32
        ).astype(jnp.bfloat16),
        "col",
        scatter_dimension=0,
        tiled=True,
    ).astype(jnp.float32)
    mixed = lax.psum_scatter(
        jnp.dot(hidden, down_weight, preferred_element_type=jnp.float32),
        "row",
        scatter_dimension=0,
        tiled=True,
    ).astype(jnp.bfloat16)
    hidden_all = lax.all_to_all(hidden, "dp", split_axis=1, concat_axis=0, tiled=True)
    cot_all = lax.all_gather(cot_full, "dp", axis=0, tiled=True)
    weight_grad = lax.dot_general(
        hidden_all, cot_all, (((0,), (0,)), ((), ())), preferred_element_type=jnp.float32
    ) / jnp.float32(lax.axis_size("dp"))
    gate_factor, up_factor = gradient_factors(gate_pre, up_pre)
    gate_grad = (hidden_share * gate_factor).astype(jnp.bfloat16)
    up_grad = (hidden_share * up_factor).astype(jnp.bfloat16)
    return (mixed, gate_grad, up_grad, weight_grad)


def solution(mesh):
    sizes = (mesh.shape["dp"], mesh.shape["row"], mesh.shape["col"])
    placed = (P("dp", "row"), P("dp", "row"), P("row", "col"), P(("dp", "row"), "col"))
    return jax.shard_map(
        body_line if sizes == (4, 2, 4) else body_general,
        mesh=mesh,
        in_specs=placed,
        out_specs=(
            P(("dp", "row"), "col"),
            P(("dp", "col"), "row"),
            P(("dp", "col"), "row"),
            P(("row", "dp"), "col"),
        ),
        check_vma=False,
    )
```

```python
import functools

import jax
import jax.numpy as jnp
from jax import lax
from jax.experimental import pallas as pl
from jax.experimental.pallas import tpu as pltpu
from jax.sharding import PartitionSpec as P

SEND_ORDER = ((3, 2, 1, 0), (2, 0, 3, 1), (1, 3, 0, 2), (0, 1, 2, 3))
ENDS = ((0, 1), (1, 0), (2, 3), (3, 2))
MIDDLE = ((1, 2), (2, 1))
ROUND_TWO = ((0, 2), (2, 3), (3, 1), (1, 0))
ROUND_THREE = ((0, 1), (1, 3), (3, 2), (2, 0))
SWAP = ((0, 1), (1, 0))
FAR = ((0, 2), (1, 3), (2, 0), (3, 1))
ACROSS = ((0, 3), (1, 2), (2, 1), (3, 0))
NEAR = ((0, 1), (1, 0), (2, 3), (3, 2))

VMEM = pl.BlockSpec(memory_space=pltpu.VMEM)
HBM = pl.BlockSpec(memory_space=pltpu.HBM)
MIB = 2**20
CHUNK = 896
WEIGHT_GRAD_PIECES = 7
NO_COST = pl.CostEstimate(flops=0, bytes_accessed=0, transcendentals=0)


def after(value, *earlier):
    return lax.optimization_barrier((value,) + earlier)[0]


def in_hbm(array):
    return pltpu.with_memory_space_constraint(array, pltpu.HBM)


def in_vmem(array):
    return pltpu.with_memory_space_constraint(array, pltpu.VMEM)


def silu_product(gate, up):
    gate = gate.astype(jnp.float32)
    return (gate * jax.nn.sigmoid(gate) * up.astype(jnp.float32)).astype(jnp.bfloat16)


def shard_columns(ref, index, shard):
    return ref.at[:, pl.ds(pl.multiple_of(index * shard, shard), shard)]


def first_kernel(
    gate_hbm, up_hbm, weight_hbm, across_ref, beside_ref, weight_ref, gate_ref, up_ref, weight_sem, gate_sems, up_sems
):
    me = lax.axis_index("dp")
    shard = gate_ref.shape[2]
    half = weight_ref.shape[0]

    def gate_copy(i):
        return pltpu.make_async_copy(
            shard_columns(gate_hbm, me ^ (3 - i), shard), gate_ref.at[i], gate_sems.at[i]
        )

    def up_copy(i):
        return pltpu.make_async_copy(
            shard_columns(up_hbm, me ^ (3 - i), shard), up_ref.at[i], up_sems.at[i]
        )

    load = pltpu.make_async_copy(weight_hbm.at[:half], weight_ref, weight_sem.at[0])
    for i in range(2):
        gate_copy(i).start()
        up_copy(i).start()
    load.start()
    for i, hidden_ref in enumerate((across_ref, beside_ref)):
        gate_copy(i).wait()
        up_copy(i).wait()
        hidden_ref[...] = silu_product(gate_ref[i], up_ref[i])
    load.wait()


def hidden_far_and_weight(gate_pre, up_pre, down_weight):
    tokens, units = gate_pre.shape
    features = down_weight.shape[1]
    shard = units // 4
    hidden = jax.ShapeDtypeStruct((tokens, shard), jnp.bfloat16)
    return pl.pallas_call(
        first_kernel,
        in_specs=[HBM] * 3,
        out_specs=[VMEM] * 3,
        out_shape=[hidden, hidden, pltpu.VMEM((units // 2, features), jnp.bfloat16)],
        scratch_shapes=[
            pltpu.VMEM((2, tokens, shard), jnp.bfloat16),
            pltpu.VMEM((2, tokens, shard), jnp.bfloat16),
            pltpu.SemaphoreType.DMA((1,)),
            pltpu.SemaphoreType.DMA((2,)),
            pltpu.SemaphoreType.DMA((2,)),
        ],
        compiler_params=pltpu.CompilerParams(vmem_limit_bytes=24 * MIB),
        cost_estimate=NO_COST,
        name="hidden_far",
    )(in_hbm(gate_pre), in_hbm(up_pre), in_hbm(down_weight))


def hidden_grad_kernel(
    own_ref, other_ref, low_ref, weight_hbm, full_ref, ends, second, third, mine, ordered_ref, high_ref, sem
):
    units = low_ref.shape[0]
    quarter = units // 2

    def load(i):
        rows = pl.ds(i * quarter, quarter)
        return pltpu.make_async_copy(
            weight_hbm.at[pl.ds(units + i * quarter, quarter)], high_ref.at[rows], sem.at[i]
        )

    load(0).start()
    load(1).start()
    half = own_ref.shape[0]
    tokens = half // 2
    top = lax.axis_index("row") == 0
    full_ref[:half] = jnp.where(top, own_ref[...], other_ref[...])
    full_ref[half:] = jnp.where(top, other_ref[...], own_ref[...])
    place = lax.axis_index("col")
    for i in range(4):
        block = jnp.int32(SEND_ORDER[0][i])
        for z in range(1, 4):
            block = jnp.where(place == z, jnp.int32(SEND_ORDER[z][i]), block)
        start = pl.multiple_of(block * tokens, tokens)
        ordered_ref[i * tokens : (i + 1) * tokens] = full_ref[pl.ds(start, tokens)]
    size = CHUNK if quarter % CHUNK == 0 else quarter
    for base, weight_ref in ((0, low_ref), (units, high_ref)):
        for start in range(0, units, size):
            if base and start % quarter == 0:
                load(start // quarter).wait()
            product = lax.dot_general(
                weight_ref[start : start + size],
                ordered_ref[...],
                (((1,), (1,)), ((), ())),
                preferred_element_type=jnp.float32,
            )
            rounded = product.astype(jnp.bfloat16).T
            columns = slice(base + start, base + start + size)
            ends[:, columns] = rounded[:tokens]
            second[:, columns] = rounded[tokens : 2 * tokens]
            third[:, columns] = rounded[2 * tokens : 3 * tokens]
            mine[:, columns] = rounded[3 * tokens :]


def hidden_grad_parts(own, other, low, down_weight):
    half, depth = own.shape
    units = low.shape[0]
    part = jax.ShapeDtypeStruct((half // 2, 2 * units), jnp.bfloat16)
    return pl.pallas_call(
        hidden_grad_kernel,
        in_specs=[VMEM, VMEM, VMEM, HBM],
        out_specs=[VMEM] * 5,
        out_shape=[jax.ShapeDtypeStruct((2 * half, depth), jnp.bfloat16)] + [part] * 4,
        scratch_shapes=[
            pltpu.VMEM((2 * half, depth), jnp.bfloat16),
            pltpu.VMEM((units, depth), jnp.bfloat16),
            pltpu.SemaphoreType.DMA((2,)),
        ],
        compiler_params=pltpu.CompilerParams(vmem_limit_bytes=24 * MIB),
        cost_estimate=NO_COST,
        name="hidden_grad",
    )(own, other, in_vmem(low), in_hbm(down_weight))


def mixed_kernel(
    gate_hbm, up_hbm, weight_hbm, across_ref, beside_ref,
    near_ref, mine_ref, keep_ref, send_ref, gate_factor_ref, up_factor_ref,
    weight_ref, gate_ref, up_ref, gate_rows_ref, up_rows_ref, total_ref,
    weight_sems, gate_sems, up_sems, row_sems,
):
    me = lax.axis_index("dp")
    tokens, shard = mine_ref.shape
    tok_rows = gate_rows_ref.shape[0]
    places = (me ^ 3, me ^ 2, me ^ 1, me)
    refs = (across_ref, beside_ref, near_ref, mine_ref)

    def gate_copy(i):
        return pltpu.make_async_copy(
            shard_columns(gate_hbm, places[2 + i], shard), gate_ref.at[i], gate_sems.at[i]
        )

    def up_copy(i):
        return pltpu.make_async_copy(
            shard_columns(up_hbm, places[2 + i], shard), up_ref.at[i], up_sems.at[i]
        )

    def weight_copy(i):
        start = pl.multiple_of(places[i] * shard, shard)
        return pltpu.make_async_copy(
            weight_hbm.at[pl.ds(start, shard)], weight_ref.at[i], weight_sems.at[i]
        )

    def row_copy(i):
        start = pl.multiple_of(lax.axis_index("col") * tok_rows, tok_rows)
        source, target = ((gate_hbm, gate_rows_ref), (up_hbm, up_rows_ref))[i]
        return pltpu.make_async_copy(source.at[pl.ds(start, tok_rows)], target, row_sems.at[i])

    for i in range(2):
        gate_copy(i).start()
        up_copy(i).start()
    for i in range(2):
        row_copy(i).start()
    for i in range(4):
        weight_copy(i).start()
    for i in range(2):
        gate_copy(i).wait()
        up_copy(i).wait()
        refs[2 + i][...] = silu_product(gate_ref[i], up_ref[i])
    row_copy(0).wait()
    row_copy(1).wait()
    units = gate_rows_ref.shape[1]
    for start in range(0, units, shard):
        columns = slice(start, start + shard)
        gate = gate_rows_ref[:, columns].astype(jnp.float32)
        sigmoid = jax.nn.sigmoid(gate)
        gate_factor_ref[:, columns] = (
            up_rows_ref[:, columns].astype(jnp.float32) * sigmoid * (1.0 + gate * (1.0 - sigmoid))
        )
        up_factor_ref[:, columns] = gate * sigmoid
    for i in range(4):
        weight_copy(i).wait()
        product = jnp.dot(refs[i][...], weight_ref[i], preferred_element_type=jnp.float32)
        if i == 0:
            total_ref[...] = product
        else:
            total_ref[...] += product
    half = tokens // 2
    row = lax.axis_index("row")
    keep_ref[...] = total_ref[pl.ds(pl.multiple_of(row * half, half), half)]
    send_ref[...] = total_ref[pl.ds(pl.multiple_of((1 - row) * half, half), half)]


def mixed_and_factors(gate_pre, up_pre, down_weight, across, beside):
    tokens, units = gate_pre.shape
    shard = units // 4
    features = down_weight.shape[1]
    tok_rows = tokens // lax.axis_size("col")
    hidden = jax.ShapeDtypeStruct((tokens, shard), jnp.bfloat16)
    partial = jax.ShapeDtypeStruct((tokens // 2, features), jnp.float32)
    factor = jax.ShapeDtypeStruct((tok_rows, units), jnp.float32)
    return pl.pallas_call(
        mixed_kernel,
        in_specs=[HBM] * 3 + [VMEM] * 2,
        out_specs=[VMEM] * 6,
        out_shape=[hidden, hidden, partial, partial, factor, factor],
        scratch_shapes=[
            pltpu.VMEM((4, shard, features), jnp.bfloat16),
            pltpu.VMEM((2, tokens, shard), jnp.bfloat16),
            pltpu.VMEM((2, tokens, shard), jnp.bfloat16),
            pltpu.VMEM((tok_rows, units), jnp.bfloat16),
            pltpu.VMEM((tok_rows, units), jnp.bfloat16),
            pltpu.VMEM((tokens, features), jnp.float32),
            pltpu.SemaphoreType.DMA((4,)),
            pltpu.SemaphoreType.DMA((2,)),
            pltpu.SemaphoreType.DMA((2,)),
            pltpu.SemaphoreType.DMA((2,)),
        ],
        compiler_params=pltpu.CompilerParams(vmem_limit_bytes=32 * MIB),
        cost_estimate=NO_COST,
        name="mixed",
    )(in_hbm(gate_pre), in_hbm(up_pre), in_hbm(down_weight), across, beside)


def weight_grad_kernel(scale, hidden_ref, cot_own, cot_far, cot_near, out_hbm, buffer, sems):
    cotangent = jnp.concatenate([cot_own[...], cot_far[...], cot_near[...]], axis=0)
    shard = hidden_ref.shape[1]
    size = shard // sems.shape[0]

    def copy_out(i):
        rows = pl.ds(i * size, size)
        return pltpu.make_async_copy(buffer.at[rows], out_hbm.at[rows], sems.at[i])

    for i in range(sems.shape[0]):
        buffer[i * size : (i + 1) * size] = lax.dot_general(
            hidden_ref[:, i * size : (i + 1) * size],
            cotangent,
            (((0,), (0,)), ((), ())),
            preferred_element_type=jnp.float32,
        ) * jnp.float32(scale)
        copy_out(i).start()
    for i in range(sems.shape[0]):
        copy_out(i).wait()


def weight_grad_shard(hidden, cot_own, cot_far, cot_near):
    shard = hidden.shape[1]
    features = cot_own.shape[1]
    pieces = WEIGHT_GRAD_PIECES if shard % (128 * WEIGHT_GRAD_PIECES) == 0 else 1
    return pl.pallas_call(
        functools.partial(weight_grad_kernel, 0.25),
        in_specs=[VMEM] * 4,
        out_specs=HBM,
        out_shape=jax.ShapeDtypeStruct((shard, features), jnp.float32),
        scratch_shapes=[
            pltpu.VMEM((shard, features), jnp.float32),
            pltpu.SemaphoreType.DMA((pieces,)),
        ],
        compiler_params=pltpu.CompilerParams(vmem_limit_bytes=24 * MIB),
        cost_estimate=NO_COST,
        name="weight_grad",
    )(hidden, cot_own, cot_far, cot_near)


def gradient_factors(gate_pre, up_pre):
    tok_rows = gate_pre.shape[0] // lax.axis_size("col")
    offset = lax.axis_index("col") * tok_rows
    gate_rows = lax.dynamic_slice_in_dim(gate_pre, offset, tok_rows, 0).astype(jnp.float32)
    up_rows = lax.dynamic_slice_in_dim(up_pre, offset, tok_rows, 0).astype(jnp.float32)
    sigmoid_rows = jax.nn.sigmoid(gate_rows)
    return (
        up_rows * sigmoid_rows * (1.0 + gate_rows * (1.0 - sigmoid_rows)),
        gate_rows * sigmoid_rows,
    )


def body_line(gate_pre, up_pre, down_weight, cotangent):
    cot_other = lax.ppermute(cotangent, "row", SWAP)
    hidden_across, hidden_beside, low = hidden_far_and_weight(gate_pre, up_pre, down_weight)

    cot_full, ends, second, third, mine = hidden_grad_parts(
        cotangent, cot_other, low, down_weight
    )
    from_end = lax.ppermute(ends, "col", ENDS)
    from_middle = lax.ppermute(ends, "col", MIDDLE)
    from_second = lax.ppermute(second, "col", ROUND_TWO)
    across = lax.ppermute(after(hidden_across, mine), "dp", ACROSS)
    beside = lax.ppermute(after(hidden_beside, mine), "dp", FAR)

    cot_far = lax.ppermute(after(cot_full, mine), "dp", FAR)
    place = lax.axis_index("col")
    transit = jnp.where((place == 1) | (place == 2), from_end, jnp.zeros_like(from_end))
    forward = (
        after(third, from_middle).astype(jnp.float32) + transit.astype(jnp.float32)
    ).astype(jnp.bfloat16)
    from_third = lax.ppermute(forward, "col", ROUND_THREE)
    hidden_near, hidden_mine, keep, send, gate_factor, up_factor = mixed_and_factors(
        gate_pre, up_pre, down_weight, after(hidden_across, cot_far, forward), hidden_beside
    )

    cot_near = lax.ppermute(jnp.concatenate([cot_full, cot_far], axis=0), "dp", NEAR)
    near = lax.ppermute(after(hidden_near, forward, beside), "dp", NEAR)
    other_half = lax.ppermute(after(send, forward).astype(jnp.bfloat16), "row", SWAP).astype(jnp.float32)
    hidden_all = lax.optimization_barrier(
        jnp.concatenate([hidden_mine, beside, near, across], axis=0)
    )
    weight_grad = weight_grad_shard(hidden_all, cot_full, cot_far, cot_near)

    mixed = (after(keep, weight_grad) + other_half).astype(jnp.bfloat16)
    so_far = (
        mine.astype(jnp.float32) + from_middle.astype(jnp.float32) + from_second.astype(jnp.float32)
    )
    so_far = lax.optimization_barrier((so_far, weight_grad))[0]
    hidden_share = so_far + after(from_third, weight_grad, mixed).astype(jnp.float32)
    gate_grad = (hidden_share * gate_factor).astype(jnp.bfloat16)
    up_grad = (hidden_share * up_factor).astype(jnp.bfloat16)
    return (mixed, gate_grad, up_grad, weight_grad)


def body_general(gate_pre, up_pre, down_weight, cotangent):
    hidden = silu_product(gate_pre, up_pre)
    cot_full = lax.all_gather(cotangent, "row", axis=0, tiled=True)
    hidden_share = lax.psum_scatter(
        lax.dot_general(
            cot_full, down_weight, (((1,), (1,)), ((), ())), preferred_element_type=jnp.float32
        ).astype(jnp.bfloat16),
        "col",
        scatter_dimension=0,
        tiled=True,
    ).astype(jnp.float32)
    mixed = lax.psum_scatter(
        jnp.dot(hidden, down_weight, preferred_element_type=jnp.float32),
        "row",
        scatter_dimension=0,
        tiled=True,
    ).astype(jnp.bfloat16)
    hidden_all = lax.all_to_all(hidden, "dp", split_axis=1, concat_axis=0, tiled=True)
    cot_all = lax.all_gather(cot_full, "dp", axis=0, tiled=True)
    weight_grad = lax.dot_general(
        hidden_all, cot_all, (((0,), (0,)), ((), ())), preferred_element_type=jnp.float32
    ) / jnp.float32(lax.axis_size("dp"))
    gate_factor, up_factor = gradient_factors(gate_pre, up_pre)
    gate_grad = (hidden_share * gate_factor).astype(jnp.bfloat16)
    up_grad = (hidden_share * up_factor).astype(jnp.bfloat16)
    return (mixed, gate_grad, up_grad, weight_grad)


def solution(mesh):
    sizes = (mesh.shape["dp"], mesh.shape["row"], mesh.shape["col"])
    placed = (P("dp", "row"), P("dp", "row"), P("row", "col"), P(("dp", "row"), "col"))
    return jax.shard_map(
        body_line if sizes == (4, 2, 4) else body_general,
        mesh=mesh,
        in_specs=placed,
        out_specs=(
            P(("dp", "row"), "col"),
            P(("dp", "col"), "row"),
            P(("dp", "col"), "row"),
            P(("row", "dp"), "col"),
        ),
        check_vma=False,
    )
```

```python
import functools

import jax
import jax.numpy as jnp
from jax import lax
from jax.experimental import pallas as pl
from jax.experimental.pallas import tpu as pltpu
from jax.sharding import PartitionSpec as P

SEND_ORDER = ((3, 2, 1, 0), (2, 0, 3, 1), (1, 3, 0, 2), (0, 1, 2, 3))
ENDS = ((0, 1), (1, 0), (2, 3), (3, 2))
MIDDLE = ((1, 2), (2, 1))
ROUND_TWO = ((0, 2), (2, 3), (3, 1), (1, 0))
ROUND_THREE = ((0, 1), (1, 3), (3, 2), (2, 0))
SWAP = ((0, 1), (1, 0))
FAR = ((0, 2), (1, 3), (2, 0), (3, 1))
ACROSS = ((0, 3), (1, 2), (2, 1), (3, 0))
NEAR = ((0, 1), (1, 0), (2, 3), (3, 2))

VMEM = pl.BlockSpec(memory_space=pltpu.VMEM)
HBM = pl.BlockSpec(memory_space=pltpu.HBM)
MIB = 2**20
CHUNK = 896
WEIGHT_GRAD_PIECES = 7
NO_COST = pl.CostEstimate(flops=0, bytes_accessed=0, transcendentals=0)


def after(value, *earlier):
    return lax.optimization_barrier((value,) + earlier)[0]


def in_hbm(array):
    return pltpu.with_memory_space_constraint(array, pltpu.HBM)


def in_vmem(array):
    return pltpu.with_memory_space_constraint(array, pltpu.VMEM)


def silu_product(gate, up):
    gate = gate.astype(jnp.float32)
    return (gate * jax.nn.sigmoid(gate) * up.astype(jnp.float32)).astype(jnp.bfloat16)


def shard_columns(ref, index, shard):
    return ref.at[:, pl.ds(pl.multiple_of(index * shard, shard), shard)]


def first_kernel(
    gate_hbm, up_hbm, weight_hbm, across_ref, beside_ref, weight_ref, gate_ref, up_ref, weight_sem, gate_sems, up_sems
):
    me = lax.axis_index("dp")
    shard = gate_ref.shape[2]
    half = weight_ref.shape[0]

    def gate_copy(i):
        return pltpu.make_async_copy(
            shard_columns(gate_hbm, me ^ (3 - i), shard), gate_ref.at[i], gate_sems.at[i]
        )

    def up_copy(i):
        return pltpu.make_async_copy(
            shard_columns(up_hbm, me ^ (3 - i), shard), up_ref.at[i], up_sems.at[i]
        )

    load = pltpu.make_async_copy(weight_hbm.at[:half], weight_ref, weight_sem.at[0])
    for i in range(2):
        gate_copy(i).start()
        up_copy(i).start()
    load.start()
    for i, hidden_ref in enumerate((across_ref, beside_ref)):
        gate_copy(i).wait()
        up_copy(i).wait()
        hidden_ref[...] = silu_product(gate_ref[i], up_ref[i])
    load.wait()


def hidden_far_and_weight(gate_pre, up_pre, down_weight):
    tokens, units = gate_pre.shape
    features = down_weight.shape[1]
    shard = units // 4
    hidden = jax.ShapeDtypeStruct((tokens, shard), jnp.bfloat16)
    return pl.pallas_call(
        first_kernel,
        in_specs=[HBM] * 3,
        out_specs=[VMEM] * 3,
        out_shape=[hidden, hidden, pltpu.VMEM((units // 2, features), jnp.bfloat16)],
        scratch_shapes=[
            pltpu.VMEM((2, tokens, shard), jnp.bfloat16),
            pltpu.VMEM((2, tokens, shard), jnp.bfloat16),
            pltpu.SemaphoreType.DMA((1,)),
            pltpu.SemaphoreType.DMA((2,)),
            pltpu.SemaphoreType.DMA((2,)),
        ],
        compiler_params=pltpu.CompilerParams(vmem_limit_bytes=24 * MIB),
        cost_estimate=NO_COST,
        name="hidden_far",
    )(in_hbm(gate_pre), in_hbm(up_pre), in_hbm(down_weight))


def hidden_grad_kernel(
    own_ref, other_ref, low_ref, weight_hbm, full_ref, ends, second, third, mine, ordered_ref, high_ref, sem
):
    units = low_ref.shape[0]
    quarter = units // 2

    def load(i):
        rows = pl.ds(i * quarter, quarter)
        return pltpu.make_async_copy(
            weight_hbm.at[pl.ds(units + i * quarter, quarter)], high_ref.at[rows], sem.at[i]
        )

    load(0).start()
    load(1).start()
    half = own_ref.shape[0]
    tokens = half // 2
    top = lax.axis_index("row") == 0
    full_ref[:half] = jnp.where(top, own_ref[...], other_ref[...])
    full_ref[half:] = jnp.where(top, other_ref[...], own_ref[...])
    place = lax.axis_index("col")
    for i in range(4):
        block = jnp.int32(SEND_ORDER[0][i])
        for z in range(1, 4):
            block = jnp.where(place == z, jnp.int32(SEND_ORDER[z][i]), block)
        start = pl.multiple_of(block * tokens, tokens)
        ordered_ref[i * tokens : (i + 1) * tokens] = full_ref[pl.ds(start, tokens)]
    size = CHUNK if quarter % CHUNK == 0 else quarter
    for base, weight_ref in ((0, low_ref), (units, high_ref)):
        for start in range(0, units, size):
            if base and start % quarter == 0:
                load(start // quarter).wait()
            product = lax.dot_general(
                weight_ref[start : start + size],
                ordered_ref[...],
                (((1,), (1,)), ((), ())),
                preferred_element_type=jnp.float32,
            )
            rounded = product.astype(jnp.bfloat16).T
            columns = slice(base + start, base + start + size)
            ends[:, columns] = rounded[:tokens]
            second[:, columns] = rounded[tokens : 2 * tokens]
            third[:, columns] = rounded[2 * tokens : 3 * tokens]
            mine[:, columns] = rounded[3 * tokens :]


def hidden_grad_parts(own, other, low, down_weight):
    half, depth = own.shape
    units = low.shape[0]
    part = jax.ShapeDtypeStruct((half // 2, 2 * units), jnp.bfloat16)
    return pl.pallas_call(
        hidden_grad_kernel,
        in_specs=[VMEM, VMEM, VMEM, HBM],
        out_specs=[VMEM] * 5,
        out_shape=[jax.ShapeDtypeStruct((2 * half, depth), jnp.bfloat16)] + [part] * 4,
        scratch_shapes=[
            pltpu.VMEM((2 * half, depth), jnp.bfloat16),
            pltpu.VMEM((units, depth), jnp.bfloat16),
            pltpu.SemaphoreType.DMA((2,)),
        ],
        compiler_params=pltpu.CompilerParams(vmem_limit_bytes=24 * MIB),
        cost_estimate=NO_COST,
        name="hidden_grad",
    )(own, other, in_vmem(low), in_hbm(down_weight))


def mixed_kernel(
    gate_hbm, up_hbm, weight_hbm, across_ref, beside_ref,
    near_ref, mine_ref, keep_ref, send_ref, gate_factor_ref, up_factor_ref,
    weight_ref, gate_ref, up_ref, gate_rows_ref, up_rows_ref, total_ref,
    weight_sems, gate_sems, up_sems, row_sems,
):
    me = lax.axis_index("dp")
    tokens, shard = mine_ref.shape
    tok_rows = gate_rows_ref.shape[0]
    places = (me ^ 3, me ^ 2, me ^ 1, me)
    refs = (across_ref, beside_ref, near_ref, mine_ref)

    def gate_copy(i):
        return pltpu.make_async_copy(
            shard_columns(gate_hbm, places[2 + i], shard), gate_ref.at[i], gate_sems.at[i]
        )

    def up_copy(i):
        return pltpu.make_async_copy(
            shard_columns(up_hbm, places[2 + i], shard), up_ref.at[i], up_sems.at[i]
        )

    def weight_copy(i):
        start = pl.multiple_of(places[i] * shard, shard)
        return pltpu.make_async_copy(
            weight_hbm.at[pl.ds(start, shard)], weight_ref.at[i], weight_sems.at[i]
        )

    def row_copy(i):
        start = pl.multiple_of(lax.axis_index("col") * tok_rows, tok_rows)
        source, target = ((gate_hbm, gate_rows_ref), (up_hbm, up_rows_ref))[i]
        return pltpu.make_async_copy(source.at[pl.ds(start, tok_rows)], target, row_sems.at[i])

    for i in range(2):
        gate_copy(i).start()
        up_copy(i).start()
    for i in range(2):
        row_copy(i).start()
    for i in range(4):
        weight_copy(i).start()
    for i in range(2):
        gate_copy(i).wait()
        up_copy(i).wait()
        refs[2 + i][...] = silu_product(gate_ref[i], up_ref[i])
    row_copy(0).wait()
    row_copy(1).wait()
    units = gate_rows_ref.shape[1]
    for start in range(0, units, shard):
        columns = slice(start, start + shard)
        gate = gate_rows_ref[:, columns].astype(jnp.float32)
        sigmoid = jax.nn.sigmoid(gate)
        gate_factor_ref[:, columns] = (
            up_rows_ref[:, columns].astype(jnp.float32) * sigmoid * (1.0 + gate * (1.0 - sigmoid))
        ).astype(jnp.bfloat16)
        up_factor_ref[:, columns] = (gate * sigmoid).astype(jnp.bfloat16)
    for i in range(4):
        weight_copy(i).wait()
        product = jnp.dot(refs[i][...], weight_ref[i], preferred_element_type=jnp.float32)
        if i == 0:
            total_ref[...] = product
        else:
            total_ref[...] += product
    half = tokens // 2
    row = lax.axis_index("row")
    keep_ref[...] = total_ref[pl.ds(pl.multiple_of(row * half, half), half)]
    send_ref[...] = total_ref[pl.ds(pl.multiple_of((1 - row) * half, half), half)]


def mixed_and_factors(gate_pre, up_pre, down_weight, across, beside):
    tokens, units = gate_pre.shape
    shard = units // 4
    features = down_weight.shape[1]
    tok_rows = tokens // lax.axis_size("col")
    hidden = jax.ShapeDtypeStruct((tokens, shard), jnp.bfloat16)
    partial = jax.ShapeDtypeStruct((tokens // 2, features), jnp.float32)
    factor = jax.ShapeDtypeStruct((tok_rows, units), jnp.bfloat16)
    return pl.pallas_call(
        mixed_kernel,
        in_specs=[HBM] * 3 + [VMEM] * 2,
        out_specs=[VMEM] * 6,
        out_shape=[hidden, hidden, partial, partial, factor, factor],
        scratch_shapes=[
            pltpu.VMEM((4, shard, features), jnp.bfloat16),
            pltpu.VMEM((2, tokens, shard), jnp.bfloat16),
            pltpu.VMEM((2, tokens, shard), jnp.bfloat16),
            pltpu.VMEM((tok_rows, units), jnp.bfloat16),
            pltpu.VMEM((tok_rows, units), jnp.bfloat16),
            pltpu.VMEM((tokens, features), jnp.float32),
            pltpu.SemaphoreType.DMA((4,)),
            pltpu.SemaphoreType.DMA((2,)),
            pltpu.SemaphoreType.DMA((2,)),
            pltpu.SemaphoreType.DMA((2,)),
        ],
        compiler_params=pltpu.CompilerParams(vmem_limit_bytes=32 * MIB),
        cost_estimate=NO_COST,
        name="mixed",
    )(in_hbm(gate_pre), in_hbm(up_pre), in_hbm(down_weight), across, beside)


def weight_grad_kernel(scale, hidden_ref, cot_own, cot_far, cot_near, out_hbm, buffer, sems):
    cotangent = jnp.concatenate([cot_own[...], cot_far[...], cot_near[...]], axis=0)
    shard = hidden_ref.shape[1]
    size = shard // sems.shape[0]

    def copy_out(i):
        rows = pl.ds(i * size, size)
        return pltpu.make_async_copy(buffer.at[rows], out_hbm.at[rows], sems.at[i])

    for i in range(sems.shape[0]):
        buffer[i * size : (i + 1) * size] = lax.dot_general(
            hidden_ref[:, i * size : (i + 1) * size],
            cotangent,
            (((0,), (0,)), ((), ())),
            preferred_element_type=jnp.float32,
        ) * jnp.float32(scale)
        copy_out(i).start()
    for i in range(sems.shape[0]):
        copy_out(i).wait()


def weight_grad_shard(hidden, cot_own, cot_far, cot_near):
    shard = hidden.shape[1]
    features = cot_own.shape[1]
    pieces = WEIGHT_GRAD_PIECES if shard % (128 * WEIGHT_GRAD_PIECES) == 0 else 1
    return pl.pallas_call(
        functools.partial(weight_grad_kernel, 0.25),
        in_specs=[VMEM] * 4,
        out_specs=HBM,
        out_shape=jax.ShapeDtypeStruct((shard, features), jnp.float32),
        scratch_shapes=[
            pltpu.VMEM((shard, features), jnp.float32),
            pltpu.SemaphoreType.DMA((pieces,)),
        ],
        compiler_params=pltpu.CompilerParams(vmem_limit_bytes=24 * MIB),
        cost_estimate=NO_COST,
        name="weight_grad",
    )(hidden, cot_own, cot_far, cot_near)


def gradient_factors(gate_pre, up_pre):
    tok_rows = gate_pre.shape[0] // lax.axis_size("col")
    offset = lax.axis_index("col") * tok_rows
    gate_rows = lax.dynamic_slice_in_dim(gate_pre, offset, tok_rows, 0).astype(jnp.float32)
    up_rows = lax.dynamic_slice_in_dim(up_pre, offset, tok_rows, 0).astype(jnp.float32)
    sigmoid_rows = jax.nn.sigmoid(gate_rows)
    return (
        up_rows * sigmoid_rows * (1.0 + gate_rows * (1.0 - sigmoid_rows)),
        gate_rows * sigmoid_rows,
    )


def body_line(gate_pre, up_pre, down_weight, cotangent):
    cot_other = lax.ppermute(cotangent, "row", SWAP)
    hidden_across, hidden_beside, low = hidden_far_and_weight(gate_pre, up_pre, down_weight)

    cot_full, ends, second, third, mine = hidden_grad_parts(
        cotangent, cot_other, low, down_weight
    )
    from_end = lax.ppermute(ends, "col", ENDS)
    from_middle = lax.ppermute(ends, "col", MIDDLE)
    from_second = lax.ppermute(second, "col", ROUND_TWO)
    across = lax.ppermute(after(hidden_across, mine), "dp", ACROSS)
    beside = lax.ppermute(after(hidden_beside, mine), "dp", FAR)

    cot_far = lax.ppermute(after(cot_full, mine), "dp", FAR)
    place = lax.axis_index("col")
    transit = jnp.where((place == 1) | (place == 2), from_end, jnp.zeros_like(from_end))
    forward = (
        after(third, from_middle).astype(jnp.float32) + transit.astype(jnp.float32)
    ).astype(jnp.bfloat16)
    from_third = lax.ppermute(forward, "col", ROUND_THREE)
    hidden_near, hidden_mine, keep, send, gate_factor, up_factor = mixed_and_factors(
        gate_pre, up_pre, down_weight, after(hidden_across, cot_far, forward), hidden_beside
    )

    cot_near = lax.ppermute(jnp.concatenate([cot_full, cot_far], axis=0), "dp", NEAR)
    near = lax.ppermute(after(hidden_near, forward, beside), "dp", NEAR)
    other_half = lax.ppermute(after(send, forward).astype(jnp.bfloat16), "row", SWAP).astype(jnp.float32)
    hidden_all = lax.optimization_barrier(
        jnp.concatenate([hidden_mine, beside, near, across], axis=0)
    )
    weight_grad = weight_grad_shard(hidden_all, cot_full, cot_far, cot_near)

    mixed = (after(keep, weight_grad) + other_half).astype(jnp.bfloat16)
    so_far = (
        mine.astype(jnp.float32) + from_middle.astype(jnp.float32) + from_second.astype(jnp.float32)
    )
    so_far = lax.optimization_barrier((so_far, weight_grad))[0]
    hidden_share = so_far + after(from_third, weight_grad, mixed).astype(jnp.float32)
    gate_grad = (hidden_share * gate_factor.astype(jnp.float32)).astype(jnp.bfloat16)
    up_grad = (hidden_share * up_factor.astype(jnp.float32)).astype(jnp.bfloat16)
    return (mixed, gate_grad, up_grad, weight_grad)


def body_general(gate_pre, up_pre, down_weight, cotangent):
    hidden = silu_product(gate_pre, up_pre)
    cot_full = lax.all_gather(cotangent, "row", axis=0, tiled=True)
    hidden_share = lax.psum_scatter(
        lax.dot_general(
            cot_full, down_weight, (((1,), (1,)), ((), ())), preferred_element_type=jnp.float32
        ).astype(jnp.bfloat16),
        "col",
        scatter_dimension=0,
        tiled=True,
    ).astype(jnp.float32)
    mixed = lax.psum_scatter(
        jnp.dot(hidden, down_weight, preferred_element_type=jnp.float32),
        "row",
        scatter_dimension=0,
        tiled=True,
    ).astype(jnp.bfloat16)
    hidden_all = lax.all_to_all(hidden, "dp", split_axis=1, concat_axis=0, tiled=True)
    cot_all = lax.all_gather(cot_full, "dp", axis=0, tiled=True)
    weight_grad = lax.dot_general(
        hidden_all, cot_all, (((0,), (0,)), ((), ())), preferred_element_type=jnp.float32
    ) / jnp.float32(lax.axis_size("dp"))
    gate_factor, up_factor = gradient_factors(gate_pre, up_pre)
    gate_grad = (hidden_share * gate_factor.astype(jnp.float32)).astype(jnp.bfloat16)
    up_grad = (hidden_share * up_factor.astype(jnp.float32)).astype(jnp.bfloat16)
    return (mixed, gate_grad, up_grad, weight_grad)


def solution(mesh):
    sizes = (mesh.shape["dp"], mesh.shape["row"], mesh.shape["col"])
    placed = (P("dp", "row"), P("dp", "row"), P("row", "col"), P(("dp", "row"), "col"))
    return jax.shard_map(
        body_line if sizes == (4, 2, 4) else body_general,
        mesh=mesh,
        in_specs=placed,
        out_specs=(
            P(("dp", "row"), "col"),
            P(("dp", "col"), "row"),
            P(("dp", "col"), "row"),
            P(("row", "dp"), "col"),
        ),
        check_vma=False,
    )
```
